512 devices in a mesh: samp: 16 (over z_hi, x), feat: 32 (over y, z_lo, core).
Axes of the slice: x: 4, y: 4, z: 16 (z_hi: 4, z_lo: 4; z = z_hi * 4 + z_lo), core: 2. Of those that a mesh axis runs over, the one named last changes fastest.
Arguments:
- design: bfloat16 [3072, 262144], P('samp', 'feat'), may hold values from -6 to 6
- weights: float32 [3072], P('samp'), may hold values from 0.01 to 0.25
- probes: bfloat16 [262144, 64], P('feat'), may hold values from -0.01171875 to 0.01171875
- barrier: float32 [262144], P(('feat', 'samp')), may hold values from 200 to 4000
Outputs:
- sketch: float32 [262144, 64], P(('feat', 'samp'))
The draws below stay inside these ranges and needn't reach their ends.
All inputs are finite; a program needn't handle non-finite values.
Results may differ from the reference program's by a relative error of at most 0.00075.
Values may be sent and summed in bfloat16 or wider, within the bound.
No kernel may reach another device: no remote copies, remote signals or barrier semaphores. Data moves between devices by JAX's collectives and lax.ppermute only.
A program may use at most 64 MiB of HBM per device.

```python
import math
import jax
import jax.numpy as jnp
from jax import lax

F = 262144
K = 64
SAMPLES = 3072


def spiked(array, rng, source, target, blocks, factor):
    def block_of(position):
        return (jnp.arange(array.shape[position]) // (array.shape[position] // blocks)).reshape((-1,) + (1,) * (array.ndim - 1 - position))

    near = jax.random.permutation(rng, blocks)[block_of(target)]
    far = (block_of(target) + blocks // 2) % blocks
    return jnp.where((block_of(source) == near) | (block_of(source) == far), factor * array, array)


def steps_of(own_key, extent, pieces, low, largest):
    level, own = 1.0, jax.random.fold_in(own_key, 6)
    for dim, parts in pieces:
        draws = jnp.exp(jax.random.uniform(jax.random.fold_in(own, dim), (parts,), jnp.float32, low / len(pieces), largest / len(pieces)))
        level = level * jnp.repeat(draws, extent[dim] // parts).reshape([-1 if axis == dim else 1 for axis in range(len(extent))])
    return level


def gaussian(rng, extent, spread, limit, split=(), kind=jnp.bfloat16):
    level = steps_of(rng, extent, split, -0.22, 0.18) if split else 1.0
    drawn = jax.random.normal(rng, extent, jnp.float32) * spread * level
    return jnp.minimum(jnp.maximum(drawn, -limit), limit).astype(kind)


def heavy_noise(stream_key, dims, spread, bound, pieces, heavy, kind=jnp.bfloat16):
    array = spread * jax.random.normal(stream_key, dims, jnp.float32)
    if pieces:
        array = array * steps_of(stream_key, dims, pieces, -0.22, 0.18)
    return jnp.clip(spiked(array, jax.random.fold_in(stream_key, 3), *heavy), -bound, bound).astype(kind)


def setup_inputs(seed: int = 0) -> dict:
    splits = jax.random.split(jax.random.key(seed), 5)
    design = heavy_noise(splits[0], (SAMPLES, F), 1.0, 6.0, ((0, 16), (1, 32)), (0, 1, 32, 2.75))
    weights = jnp.clip(jnp.exp(math.log(0.25) - 3.218876 * jax.random.uniform(splits[1], (SAMPLES,), jnp.float32) ** steps_of(splits[1], (SAMPLES,), ((0, 16),), -0.2, 0.2)), 0.01, 0.25)
    probes = gaussian(splits[2], (F, K), F ** -0.5, 0.01171875, ((0, 32),))
    barrier = jnp.clip(jnp.exp(math.log(4000.0) - 2.9957323 * jax.random.uniform(splits[3], (F,), jnp.float32) ** steps_of(splits[3], (F,), ((0, 512),), -0.2, 0.2)), 200.0, 4000.0)
    return {"design": design, "weights": weights, "probes": probes, "barrier": barrier}


def reference(design, weights, probes, barrier):
    projected = jnp.dot(design, probes, preferred_element_type=jnp.float32)
    scaled = (weights[:, None] * projected).astype(jnp.bfloat16)
    hessian = lax.dot_general(design, scaled, (((0,), (0,)), ((), ())), preferred_element_type=jnp.float32)
    return hessian + barrier[:, None] * probes.astype(jnp.float32)
```

```python
import jax
import jax.numpy as jnp
from jax import lax
from jax.sharding import PartitionSpec as P

X = 4
Z = 4
DESIGN_MAX = 6.0
WEIGHT_MAX = 0.25
F16_TOP = 32768.0

X_GROUPS = [[z * X + x for x in range(X)] for z in range(Z)]
Z_GROUPS = [[z * X + x for z in range(Z)] for x in range(X)]


def per_device(design, weights, probes, barrier):
    samples, feats = design.shape
    columns = probes.shape[1]
    n_feat = lax.axis_size("feat")
    feat = lax.axis_index("feat")
    owned = feats // (X * Z)
    half = samples // 2
    rows = half // n_feat
    probes_t = probes.T

    partial = jnp.dot(design, probes, preferred_element_type=jnp.float32)
    packed = jnp.concatenate([partial[:half], partial[half:]], axis=1).reshape(n_feat, rows, 2 * columns)
    mass = jnp.sum(jnp.abs(probes_t.astype(jnp.float32)), axis=1)
    mass = jnp.concatenate([mass, mass])
    sent = jnp.concatenate([packed, jnp.broadcast_to(mass, (n_feat, 1, 2 * columns))], axis=1)
    got = lax.all_to_all(sent, "feat", 0, 0).sum(0)
    projected, total_mass = got[:rows], got[rows, :columns]

    low = lax.dynamic_slice_in_dim(weights, feat * rows, rows, 0)
    high = lax.dynamic_slice_in_dim(weights, half + feat * rows, rows, 0)
    factor = jnp.concatenate(
        [jnp.broadcast_to(low[:, None], (rows, columns)), jnp.broadcast_to(high[:, None], (rows, columns))], axis=1
    )
    own = (factor * projected).astype(jnp.bfloat16)
    gathered = lax.all_to_all(jnp.broadcast_to(own, (n_feat, rows, 2 * columns)), "feat", 0, 0)
    gathered = gathered.reshape(half, 2 * columns)
    scaled = jnp.concatenate([gathered[:, :columns], gathered[:, columns:]], axis=0)

    bound = (X * samples) * DESIGN_MAX * WEIGHT_MAX * DESIGN_MAX * jnp.maximum(total_mass, 1e-30)[:, None]
    down, up = F16_TOP / bound, bound / F16_TOP
    hessian = lax.dot_general(scaled, design, (((0,), (0,)), ((), ())), preferred_element_type=jnp.float32)
    sent = (hessian * down).astype(jnp.float16).reshape(columns, Z, X, owned).transpose(2, 1, 0, 3)
    got = lax.all_to_all(sent, "samp", 0, 0, axis_index_groups=X_GROUPS)
    sent = got.astype(jnp.float32).sum(0).astype(jnp.float16)
    got = lax.all_to_all(sent, "samp", 0, 0, axis_index_groups=Z_GROUPS)
    summed = got.astype(jnp.float32).sum(0) * up

    own_probes = lax.dynamic_slice_in_dim(probes_t, lax.axis_index("samp") * owned, owned, 1)
    return (summed + barrier[None, :] * own_probes.astype(jnp.float32)).T


def solution(mesh):
    placed = (P("samp", "feat"), P("samp"), P("feat", None), P(("feat", "samp")))
    return jax.shard_map(
        per_device, mesh=mesh, in_specs=placed, out_specs=P(("feat", "samp"), None), check_vma=False
    )
```

```python
import jax
import jax.numpy as jnp
from jax import lax
from jax.experimental import pallas as pl
from jax.experimental.pallas import tpu as pltpu
from jax.sharding import PartitionSpec as P

X = 4
Z = 4
DESIGN_MAX = 6.0
WEIGHT_MAX = 0.25
F16_TOP = 32768.0

X_GROUPS = [[z * X + x for x in range(X)] for z in range(Z)]
Z_GROUPS = [[z * X + x for z in range(Z)] for x in range(X)]


def project_kernel(design_ref, probes_ref, packed_ref, mass_ref, total, mass):
    step = pl.program_id(0)
    probes = probes_ref[...]
    contract = (((1,), (1,)), ((), ()))
    part = lax.dot_general(design_ref[...], probes, contract, preferred_element_type=jnp.float32)
    ones = jnp.ones((8, probes.shape[1]), jnp.bfloat16)
    part_mass = lax.dot_general(ones, jnp.abs(probes), contract, preferred_element_type=jnp.float32)

    @pl.when(step == 0)
    def _():
        total[...] = part
        mass[...] = part_mass

    @pl.when(step > 0)
    def _():
        total[...] += part
        mass[...] += part_mass

    @pl.when(step == pl.num_programs(0) - 1)
    def _():
        half = total.shape[0] // 2
        packed_ref[...] = jnp.concatenate([total[:half], total[half:]], axis=1)
        mass_ref[...] = jnp.concatenate([mass[...], mass[...]], axis=1)


def project(design, probes_t):
    samples, feats = design.shape
    columns = probes_t.shape[0]
    block = 2048
    return pl.pallas_call(
        project_kernel,
        grid=(feats // block,),
        in_specs=[
            pl.BlockSpec((samples, block), lambda i: (0, i)),
            pl.BlockSpec((columns, block), lambda i: (0, i)),
        ],
        out_specs=[
            pl.BlockSpec((samples // 2, 2 * columns), lambda i: (0, 0)),
            pl.BlockSpec((8, 2 * columns), lambda i: (0, 0)),
        ],
        out_shape=[
            jax.ShapeDtypeStruct((samples // 2, 2 * columns), jnp.float32),
            jax.ShapeDtypeStruct((8, 2 * columns), jnp.float32),
        ],
        scratch_shapes=[
            pltpu.VMEM((samples, columns), jnp.float32),
            pltpu.VMEM((8, columns), jnp.float32),
        ],
        compiler_params=pltpu.CompilerParams(vmem_limit_bytes=60 * 1024 * 1024),
        cost_estimate=pl.CostEstimate(
            flops=2 * samples * feats * columns, bytes_accessed=2 * feats * (samples + columns), transcendentals=0
        ),
    )(design, probes_t)


def sketch_kernel(gathered_ref, mass_ref, design_ref, out_ref):
    columns = out_ref.shape[2]
    owned = out_ref.shape[3]
    gathered = gathered_ref[...]
    scaled = jnp.concatenate([gathered[:, :columns], gathered[:, columns:]], axis=0)
    row = jnp.broadcast_to(mass_ref[...][:1, :columns], (columns, columns))
    same = lax.broadcasted_iota(jnp.int32, row.shape, 0) == lax.broadcasted_iota(jnp.int32, row.shape, 1)
    mass = jnp.sum(jnp.where(same, row, 0.0), axis=1, keepdims=True)
    down = F16_TOP / size_bound(mass, scaled.shape[0])
    for z in range(Z):
        for x in range(X):
            at = (z * X + x) * owned
            part = lax.dot_general(
                scaled, design_ref[:, at : at + owned], (((0,), (0,)), ((), ())), preferred_element_type=jnp.float32
            )
            out_ref[x, z] = part * down


def sketch_parts(gathered, mass, design):
    samples, feats = design.shape
    columns = gathered.shape[1] // 2
    return pl.pallas_call(
        sketch_kernel,
        out_shape=jax.ShapeDtypeStruct((X, Z, columns, feats // (X * Z)), jnp.float32),
        in_specs=[pl.BlockSpec(memory_space=pltpu.VMEM)] * 3,
        out_specs=pl.BlockSpec(memory_space=pltpu.VMEM),
        compiler_params=pltpu.CompilerParams(vmem_limit_bytes=16 * 1024 * 1024),
        cost_estimate=pl.CostEstimate(
            flops=2 * samples * feats * columns, bytes_accessed=2 * feats * (samples + 2 * columns), transcendentals=0
        ),
    )(gathered, mass, design)


def size_bound(mass, samples):
    return (X * samples * DESIGN_MAX * WEIGHT_MAX * DESIGN_MAX) * jnp.maximum(mass, 1e-30)


def per_device(design, weights, probes, barrier):
    samples, feats = design.shape
    columns = probes.shape[1]
    n_feat = lax.axis_size("feat")
    feat = lax.axis_index("feat")
    owned = feats // (X * Z)
    half = samples // 2
    rows = half // n_feat
    probes_t = probes.T

    packed, mass = project(design, probes_t)
    packed = packed.reshape(n_feat, rows, 2 * columns)
    sent = jnp.concatenate([packed, jnp.broadcast_to(mass[:1], (n_feat, 1, 2 * columns))], axis=1)
    got = lax.all_to_all(sent, "feat", 0, 0).sum(0)
    projected, total_mass = got[:rows], got[rows:]

    low = lax.dynamic_slice_in_dim(weights, feat * rows, rows, 0)
    high = lax.dynamic_slice_in_dim(weights, half + feat * rows, rows, 0)
    factor = jnp.concatenate(
        [jnp.broadcast_to(low[:, None], (rows, columns)), jnp.broadcast_to(high[:, None], (rows, columns))], axis=1
    )
    own = (factor * projected).astype(jnp.bfloat16)
    gathered = lax.all_to_all(jnp.broadcast_to(own, (n_feat, rows, 2 * columns)), "feat", 0, 0)
    gathered = gathered.reshape(half, 2 * columns)

    up = size_bound(total_mass[0, :columns], samples)[:, None] / F16_TOP
    own_probes = lax.dynamic_slice_in_dim(probes_t, lax.axis_index("samp") * owned, owned, 1)
    diagonal = barrier[None, :] * own_probes.astype(jnp.float32)
    up = jnp.broadcast_to(up, diagonal.shape)
    gathered, diagonal, up = lax.optimization_barrier((gathered, diagonal, up))

    sent = sketch_parts(gathered, total_mass, design).astype(jnp.float16)
    got = lax.all_to_all(sent, "samp", 0, 0, axis_index_groups=X_GROUPS)
    sent = got.astype(jnp.float32).sum(0).astype(jnp.float16)
    got = lax.all_to_all(sent, "samp", 0, 0, axis_index_groups=Z_GROUPS)
    return (got.astype(jnp.float32).sum(0) * up + diagonal).T


def solution(mesh):
    placed = (P("samp", "feat"), P("samp"), P("feat", None), P(("feat", "samp")))
    return jax.shard_map(
        per_device, mesh=mesh, in_specs=placed, out_specs=P(("feat", "samp"), None), check_vma=False
    )
```

```python
import jax
import jax.numpy as jnp
from jax import lax
from jax.experimental import pallas as pl
from jax.experimental.pallas import tpu as pltpu
from jax.sharding import PartitionSpec as P

X = 4
Y = 4
Z = 4
CORES = 2
CHUNKS = 8
DESIGN_MAX = 6.0
WEIGHT_MAX = 0.25
F16_TOP = 32768.0

X_GROUPS = [[z * X + x for x in range(X)] for z in range(Z)]
Z_GROUPS = [[z * X + x for z in range(Z)] for x in range(X)]
YC_GROUPS = [[(y * Z + z) * CORES + c for y in range(Y) for c in range(CORES)] for z in range(Z)]
ZLO_GROUPS = [[(y * Z + z) * CORES + c for z in range(Z)] for y in range(Y) for c in range(CORES)]

VMEM = pl.BlockSpec(memory_space=pltpu.VMEM)


def row_of(column):
    n = column.shape[0]
    same = lax.broadcasted_iota(jnp.int32, (n, n), 0) == lax.broadcasted_iota(jnp.int32, (n, n), 1)
    return jnp.sum(jnp.where(same, jnp.broadcast_to(column, (n, n)), 0.0), axis=0, keepdims=True)


def column_of(row):
    n = row.shape[1]
    same = lax.broadcasted_iota(jnp.int32, (n, n), 0) == lax.broadcasted_iota(jnp.int32, (n, n), 1)
    return jnp.sum(jnp.where(same, jnp.broadcast_to(row, (n, n)), 0.0), axis=1, keepdims=True)


def project_kernel(design_ref, probes_ref, out_ref, design_buf, probes_buf, sems):
    width = design_ref.shape[1] // CHUNKS
    copies = []
    for i in range(CHUNKS):
        at = pl.ds(i * width, width)
        pair = [
            pltpu.make_async_copy(probes_ref.at[:, at], probes_buf.at[:, at], sems.at[0, i]),
            pltpu.make_async_copy(design_ref.at[:, at], design_buf.at[:, at], sems.at[1, i]),
        ]
        for copy in pair:
            copy.start()
        copies.append(pair)
    total, mass = 0.0, 0.0
    for i in range(CHUNKS):
        for copy in copies[i]:
            copy.wait()
        design = design_buf[:, i * width : (i + 1) * width]
        probes = probes_buf[:, i * width : (i + 1) * width]
        total += lax.dot_general(design, probes, (((1,), (1,)), ((), ())), preferred_element_type=jnp.float32)
        size = jnp.abs(probes).astype(jnp.float32)
        for j in range(width // 128):
            mass += size[:, j * 128 : (j + 1) * 128]
    half = total.shape[0] // 2
    packed = jnp.concatenate([total[:half], total[half:]], axis=1)
    row = row_of(jnp.sum(mass, axis=1, keepdims=True))
    row = jnp.broadcast_to(jnp.concatenate([row, row], axis=1), (8, packed.shape[1]))
    for i in range(out_ref.shape[0]):
        out_ref[i, :half] = packed
        out_ref[i, half:] = row


def project(design, probes_t):
    samples, feats = design.shape
    columns = probes_t.shape[0]
    return pl.pallas_call(
        project_kernel,
        in_specs=[pl.BlockSpec(memory_space=pl.ANY)] * 2,
        out_specs=VMEM,
        out_shape=jax.ShapeDtypeStruct((Y * CORES, samples // 2 + 8, 2 * columns), jnp.float32),
        scratch_shapes=[
            pltpu.VMEM((samples, feats), jnp.bfloat16),
            pltpu.VMEM((columns, feats), jnp.bfloat16),
            pltpu.SemaphoreType.DMA((2, CHUNKS)),
        ],
        compiler_params=pltpu.CompilerParams(vmem_limit_bytes=60 * 1024 * 1024),
        cost_estimate=pl.CostEstimate(
            flops=2 * samples * feats * columns, bytes_accessed=2 * feats * (samples + columns), transcendentals=0
        ),
    )(design, probes_t)


def resum_kernel(in_ref, out_ref):
    total = in_ref[0]
    for i in range(1, in_ref.shape[0]):
        total += in_ref[i]
    for i in range(out_ref.shape[0]):
        out_ref[i] = total


def resum(parts):
    shape = (Z,) + parts.shape[1:]
    return pl.pallas_call(
        resum_kernel,
        in_specs=[VMEM],
        out_specs=VMEM,
        out_shape=jax.ShapeDtypeStruct(shape, jnp.float32),
        compiler_params=pltpu.CompilerParams(vmem_limit_bytes=8 * 1024 * 1024),
        cost_estimate=pl.CostEstimate(flops=parts.size, bytes_accessed=6 * parts.size, transcendentals=0),
    )(parts)


def sketch_kernel(parts_ref, factor_ref, design_ref, out_ref, up_ref):
    columns, owned = out_ref.shape[2:]
    half = factor_ref.shape[0]
    total = parts_ref[0]
    for i in range(1, parts_ref.shape[0]):
        total += parts_ref[i]
    scaled = (factor_ref[...] * total[:half]).astype(jnp.bfloat16)
    scaled = jnp.concatenate([scaled[:, :columns], scaled[:, columns:]], axis=0)
    mass = column_of(total[half : half + 1, :columns])
    bound = (X * 2 * half * DESIGN_MAX * WEIGHT_MAX * DESIGN_MAX) * jnp.maximum(mass, 1e-30)
    down = F16_TOP / bound
    up_ref[...] = jnp.broadcast_to(bound / F16_TOP, up_ref.shape)
    for z in range(Z):
        for x in range(X):
            at = (z * X + x) * owned
            part = lax.dot_general(
                scaled, design_ref[:, at : at + owned], (((0,), (0,)), ((), ())), preferred_element_type=jnp.float32
            )
            out_ref[x, z] = part * down


def sketch_parts(parts, factor, design):
    samples, feats = design.shape
    columns = parts.shape[2] // 2
    owned = feats // (X * Z)
    return pl.pallas_call(
        sketch_kernel,
        in_specs=[VMEM] * 3,
        out_specs=[VMEM] * 2,
        out_shape=[
            jax.ShapeDtypeStruct((X, Z, columns, owned), jnp.float32),
            jax.ShapeDtypeStruct((columns, owned), jnp.float32),
        ],
        compiler_params=pltpu.CompilerParams(vmem_limit_bytes=16 * 1024 * 1024),
        cost_estimate=pl.CostEstimate(
            flops=2 * samples * feats * columns, bytes_accessed=2 * feats * (samples + 2 * columns), transcendentals=0
        ),
    )(parts, factor, design)


def per_device(design, weights, probes, barrier):
    samples, feats = design.shape
    columns = probes.shape[1]
    owned = feats // (X * Z)
    half = samples // 2
    probes_t = probes.T

    own_probes = lax.dynamic_slice_in_dim(probes_t, lax.axis_index("samp") * owned, owned, 1)
    diagonal = barrier[None, :] * own_probes.astype(jnp.float32)
    factor = jnp.concatenate([jnp.broadcast_to(w[:, None], (half, columns)) for w in (weights[:half], weights[half:])], axis=1)

    parts = lax.all_to_all(project(design, probes_t), "feat", 0, 0, axis_index_groups=YC_GROUPS)
    parts = lax.all_to_all(resum(parts), "feat", 0, 0, axis_index_groups=ZLO_GROUPS)
    parts, factor, diagonal = lax.optimization_barrier((parts, factor, diagonal))

    sent, up = sketch_parts(parts, factor, design)
    got = lax.all_to_all(sent.astype(jnp.float16), "samp", 0, 0, axis_index_groups=X_GROUPS)
    sent = got.astype(jnp.float32).sum(0).astype(jnp.float16)
    got = lax.all_to_all(sent, "samp", 0, 0, axis_index_groups=Z_GROUPS)
    return (got.astype(jnp.float32).sum(0) * up + diagonal).T


def solution(mesh):
    placed = (P("samp", "feat"), P("samp"), P("feat", None), P(("feat", "samp")))
    return jax.shard_map(
        per_device, mesh=mesh, in_specs=placed, out_specs=P(("feat", "samp"), None), check_vma=False
    )
```

```python
import jax
import jax.numpy as jnp
from jax import lax
from jax.experimental import pallas as pl
from jax.experimental.pallas import tpu as pltpu
from jax.sharding import PartitionSpec as P

X = 4
Y = 4
Z = 4
CORES = 2
CHUNKS = 8
DESIGN_MAX = 6.0
WEIGHT_MAX = 0.25
F16_TOP = 32768.0

X_GROUPS = [[z * X + x for x in range(X)] for z in range(Z)]
FAR_FIRST = (2, 1, 3)
YC_GROUPS = [[(y * Z + z) * CORES + c for y in range(Y) for c in range(CORES)] for z in range(Z)]
ZLO_GROUPS = [[(y * Z + z) * CORES + c for z in range(Z)] for y in range(Y) for c in range(CORES)]

VMEM = pl.BlockSpec(memory_space=pltpu.VMEM)


def row_of(column):
    n = column.shape[0]
    same = lax.broadcasted_iota(jnp.int32, (n, n), 0) == lax.broadcasted_iota(jnp.int32, (n, n), 1)
    return jnp.sum(jnp.where(same, jnp.broadcast_to(column, (n, n)), 0.0), axis=0, keepdims=True)


def column_of(row):
    n = row.shape[1]
    same = lax.broadcasted_iota(jnp.int32, (n, n), 0) == lax.broadcasted_iota(jnp.int32, (n, n), 1)
    return jnp.sum(jnp.where(same, jnp.broadcast_to(row, (n, n)), 0.0), axis=1, keepdims=True)


def project_kernel(design_ref, probes_ref, out_ref, design_buf, probes_buf, sems):
    width = design_ref.shape[1] // CHUNKS
    copies = []
    for i in range(CHUNKS):
        at = pl.ds(i * width, width)
        pair = [
            pltpu.make_async_copy(probes_ref.at[:, at], probes_buf.at[:, at], sems.at[0, i]),
            pltpu.make_async_copy(design_ref.at[:, at], design_buf.at[:, at], sems.at[1, i]),
        ]
        for copy in pair:
            copy.start()
        copies.append(pair)
    total, mass = 0.0, 0.0
    for i in range(CHUNKS):
        for copy in copies[i]:
            copy.wait()
        design = design_buf[:, i * width : (i + 1) * width]
        probes = probes_buf[:, i * width : (i + 1) * width]
        total += lax.dot_general(design, probes, (((1,), (1,)), ((), ())), preferred_element_type=jnp.float32)
        size = jnp.abs(probes).astype(jnp.float32)
        for j in range(width // 128):
            mass += size[:, j * 128 : (j + 1) * 128]
    half = total.shape[0] // 2
    packed = jnp.concatenate([total[:half], total[half:]], axis=1)
    row = row_of(jnp.sum(mass, axis=1, keepdims=True))
    row = jnp.broadcast_to(jnp.concatenate([row, row], axis=1), (8, packed.shape[1]))
    for i in range(out_ref.shape[0]):
        out_ref[i, :half] = packed
        out_ref[i, half:] = row


def project(design, probes_t):
    samples, feats = design.shape
    columns = probes_t.shape[0]
    return pl.pallas_call(
        project_kernel,
        in_specs=[pl.BlockSpec(memory_space=pl.ANY)] * 2,
        out_specs=VMEM,
        out_shape=jax.ShapeDtypeStruct((Y * CORES, samples // 2 + 8, 2 * columns), jnp.float32),
        scratch_shapes=[
            pltpu.VMEM((samples, feats), jnp.bfloat16),
            pltpu.VMEM((columns, feats), jnp.bfloat16),
            pltpu.SemaphoreType.DMA((2, CHUNKS)),
        ],
        compiler_params=pltpu.CompilerParams(vmem_limit_bytes=60 * 1024 * 1024),
        cost_estimate=pl.CostEstimate(
            flops=2 * samples * feats * columns, bytes_accessed=2 * feats * (samples + columns), transcendentals=0
        ),
    )(design, probes_t)


def resum_kernel(in_ref, out_ref):
    total = in_ref[0]
    for i in range(1, in_ref.shape[0]):
        total += in_ref[i]
    for i in range(out_ref.shape[0]):
        out_ref[i] = total


def resum(parts):
    shape = (Z,) + parts.shape[1:]
    return pl.pallas_call(
        resum_kernel,
        in_specs=[VMEM],
        out_specs=VMEM,
        out_shape=jax.ShapeDtypeStruct(shape, jnp.float32),
        compiler_params=pltpu.CompilerParams(vmem_limit_bytes=8 * 1024 * 1024),
        cost_estimate=pl.CostEstimate(flops=parts.size, bytes_accessed=6 * parts.size, transcendentals=0),
    )(parts)


def sketch_kernel(own_z, parts_ref, factor_ref, design_ref, out_ref, up_ref):
    columns, owned = out_ref.shape[2:]
    half = factor_ref.shape[0]
    total = parts_ref[0]
    for i in range(1, parts_ref.shape[0]):
        total += parts_ref[i]
    scaled = (factor_ref[...] * total[:half]).astype(jnp.bfloat16)
    scaled = jnp.concatenate([scaled[:, :columns], scaled[:, columns:]], axis=0)
    mass = column_of(total[half : half + 1, :columns])
    bound = (X * 2 * half * DESIGN_MAX * WEIGHT_MAX * DESIGN_MAX) * jnp.maximum(mass, 1e-30)
    down = F16_TOP / bound
    up_ref[...] = jnp.broadcast_to(bound / F16_TOP, up_ref.shape)
    for z in range(Z):
        for x in range(X):
            at = (z * X + x) * owned
            part = lax.dot_general(
                scaled, design_ref[:, at : at + owned], (((0,), (0,)), ((), ())), preferred_element_type=jnp.float32
            )
            out_ref[x, lax.rem(z + Z - own_z[0], Z)] = part * down


def sketch_parts(parts, factor, design):
    samples, feats = design.shape
    columns = parts.shape[2] // 2
    owned = feats // (X * Z)
    return pl.pallas_call(
        sketch_kernel,
        in_specs=[pl.BlockSpec(memory_space=pltpu.SMEM)] + [VMEM] * 3,
        out_specs=[VMEM] * 2,
        out_shape=[
            jax.ShapeDtypeStruct((X, Z, columns, owned), jnp.float32),
            jax.ShapeDtypeStruct((columns, owned), jnp.float32),
        ],
        compiler_params=pltpu.CompilerParams(vmem_limit_bytes=16 * 1024 * 1024),
        cost_estimate=pl.CostEstimate(
            flops=2 * samples * feats * columns, bytes_accessed=2 * feats * (samples + 2 * columns), transcendentals=0
        ),
    )((lax.axis_index("samp") // X).reshape(1), parts, factor, design)


def per_device(design, weights, probes, barrier):
    samples, feats = design.shape
    columns = probes.shape[1]
    owned = feats // (X * Z)
    half = samples // 2
    probes_t = probes.T

    own_probes = lax.dynamic_slice_in_dim(probes_t, lax.axis_index("samp") * owned, owned, 1)
    diagonal = barrier[None, :] * own_probes.astype(jnp.float32)
    factor = jnp.concatenate([jnp.broadcast_to(w[:, None], (half, columns)) for w in (weights[:half], weights[half:])], axis=1)

    parts = lax.all_to_all(project(design, probes_t), "feat", 0, 0, axis_index_groups=YC_GROUPS)
    parts = lax.all_to_all(resum(parts), "feat", 0, 0, axis_index_groups=ZLO_GROUPS)
    parts, factor, diagonal = lax.optimization_barrier((parts, factor, diagonal))

    sent, up = sketch_parts(parts, factor, design)
    got = lax.all_to_all(sent.astype(jnp.float16), "samp", 0, 0, axis_index_groups=X_GROUPS)
    sent = got.astype(jnp.float32).sum(0).astype(jnp.float16)
    total = sent[0].astype(jnp.float32)
    for far in FAR_FIRST:
        step = [(z * X + x, (z + far) % Z * X + x) for z in range(Z) for x in range(X)]
        total += lax.ppermute(sent[far], "samp", step).astype(jnp.float32)
    return (total * up + diagonal).T


def solution(mesh):
    placed = (P("samp", "feat"), P("samp"), P("feat", None), P(("feat", "samp")))
    return jax.shard_map(
        per_device, mesh=mesh, in_specs=placed, out_specs=P(("feat", "samp"), None), check_vma=False
    )
```

```python
import jax
import jax.numpy as jnp
from jax import lax
from jax.experimental import pallas as pl
from jax.experimental.pallas import tpu as pltpu
from jax.sharding import PartitionSpec as P

X = 4
Y = 4
Z = 4
CORES = 2
CHUNKS = 2
DESIGN_MAX = 6.0
WEIGHT_MAX = 0.25
F16_TOP = 32768.0

X_GROUPS = [[z * X + x for x in range(X)] for z in range(Z)]
FAR_FIRST = (2, 1, 3)
YC_GROUPS = [[(y * Z + z) * CORES + c for y in range(Y) for c in range(CORES)] for z in range(Z)]
ZLO_GROUPS = [[(y * Z + z) * CORES + c for z in range(Z)] for y in range(Y) for c in range(CORES)]

VMEM = pl.BlockSpec(memory_space=pltpu.VMEM)


def row_of(column):
    n = column.shape[0]
    same = lax.broadcasted_iota(jnp.int32, (n, n), 0) == lax.broadcasted_iota(jnp.int32, (n, n), 1)
    return jnp.sum(jnp.where(same, jnp.broadcast_to(column, (n, n)), 0.0), axis=0, keepdims=True)


def column_of(row):
    n = row.shape[1]
    same = lax.broadcasted_iota(jnp.int32, (n, n), 0) == lax.broadcasted_iota(jnp.int32, (n, n), 1)
    return jnp.sum(jnp.where(same, jnp.broadcast_to(row, (n, n)), 0.0), axis=1, keepdims=True)


def project_kernel(own, barrier_ref, design_ref, probes_ref, out_ref, diagonal_ref, total, mass):
    step = pl.program_id(0)
    width = probes_ref.shape[1]
    half, owned = total.shape[0] // 2, diagonal_ref.shape[1]

    @pl.when(step == 0)
    def _():
        total[...] = jnp.zeros_like(total)
        mass[...] = jnp.zeros_like(mass)

    total[...] += lax.dot_general(
        design_ref[...], probes_ref[...], (((1,), (1,)), ((), ())), preferred_element_type=jnp.float32
    )
    size = jnp.abs(probes_ref[...]).astype(jnp.float32)
    for j in range(width // 128):
        mass[...] += size[:, j * 128 : (j + 1) * 128]

    blocks = width // owned

    @pl.when(step == lax.div(own[0], blocks))
    def _():
        at = pl.multiple_of(lax.rem(own[0], blocks) * owned, owned)
        diagonal_ref[...] = barrier_ref[...] * probes_ref[:, pl.ds(at, owned)].astype(jnp.float32)

    @pl.when(step == pl.num_programs(0) - 1)
    def _():
        packed = jnp.concatenate([total[:half], total[half:]], axis=1)
        row = row_of(jnp.sum(mass[...], axis=1, keepdims=True))
        row = jnp.broadcast_to(jnp.concatenate([row, row], axis=1), (8, packed.shape[1]))
        for i in range(out_ref.shape[0]):
            out_ref[i, :half] = packed
            out_ref[i, half:] = row


def project(own, barrier, design, probes_t):
    samples, feats = design.shape
    columns, owned = probes_t.shape[0], barrier.shape[1]
    half, width = samples // 2, feats // CHUNKS
    return pl.pallas_call(
        project_kernel,
        grid=(CHUNKS,),
        in_specs=[
            pl.BlockSpec(memory_space=pltpu.SMEM),
            pl.BlockSpec((1, owned), lambda i: (0, 0)),
            pl.BlockSpec((samples, width), lambda i: (0, i)),
            pl.BlockSpec((columns, width), lambda i: (0, i)),
        ],
        out_specs=[
            pl.BlockSpec((Y * CORES, half + 8, 2 * columns), lambda i: (0, 0, 0)),
            pl.BlockSpec((columns, owned), lambda i: (0, 0)),
        ],
        out_shape=[
            jax.ShapeDtypeStruct((Y * CORES, half + 8, 2 * columns), jnp.float32),
            jax.ShapeDtypeStruct((columns, owned), jnp.float32),
        ],
        scratch_shapes=[pltpu.VMEM((samples, columns), jnp.float32), pltpu.VMEM((columns, 128), jnp.float32)],
        compiler_params=pltpu.CompilerParams(vmem_limit_bytes=60 * 1024 * 1024),
        cost_estimate=pl.CostEstimate(
            flops=2 * samples * feats * columns, bytes_accessed=2 * feats * (samples + columns), transcendentals=0
        ),
    )(own, barrier, design, probes_t)


def resum_kernel(in_ref, out_ref):
    total = in_ref[0]
    for i in range(1, in_ref.shape[0]):
        total += in_ref[i]
    for i in range(out_ref.shape[0]):
        out_ref[i] = total


def resum(parts):
    shape = (Z,) + parts.shape[1:]
    return pl.pallas_call(
        resum_kernel,
        in_specs=[VMEM],
        out_specs=VMEM,
        out_shape=jax.ShapeDtypeStruct(shape, jnp.float32),
        compiler_params=pltpu.CompilerParams(vmem_limit_bytes=8 * 1024 * 1024),
        cost_estimate=pl.CostEstimate(flops=parts.size, bytes_accessed=6 * parts.size, transcendentals=0),
    )(parts)


def sketch_kernel(own, weights_ref, parts_ref, design_ref, out_ref, up_ref):
    columns, owned = out_ref.shape[2:]
    half = design_ref.shape[0] // 2
    own_z = lax.div(own[0], X)
    total = parts_ref[0]
    for i in range(1, parts_ref.shape[0]):
        total += parts_ref[i]
    projected = jnp.concatenate([total[:half, :columns], total[:half, columns:]], axis=0)
    scaled = (column_of(weights_ref[...]) * projected).astype(jnp.bfloat16)
    mass = column_of(total[half : half + 1, :columns])
    bound = (X * 2 * half * DESIGN_MAX * WEIGHT_MAX * DESIGN_MAX) * jnp.maximum(mass, 1e-30)
    down = F16_TOP / bound
    up_ref[...] = jnp.broadcast_to(bound / F16_TOP, up_ref.shape)
    for z in range(Z):
        for x in range(X):
            at = (z * X + x) * owned
            part = lax.dot_general(
                scaled, design_ref[:, at : at + owned], (((0,), (0,)), ((), ())), preferred_element_type=jnp.float32
            )
            out_ref[x, lax.rem(z + Z - own_z, Z)] = part * down


def sketch_parts(own, weights, parts, design):
    samples, feats = design.shape
    columns = parts.shape[2] // 2
    owned = feats // (X * Z)
    return pl.pallas_call(
        sketch_kernel,
        in_specs=[pl.BlockSpec(memory_space=pltpu.SMEM)] + [VMEM] * 3,
        out_specs=[VMEM] * 2,
        out_shape=[
            jax.ShapeDtypeStruct((X, Z, columns, owned), jnp.float32),
            jax.ShapeDtypeStruct((columns, owned), jnp.float32),
        ],
        compiler_params=pltpu.CompilerParams(vmem_limit_bytes=16 * 1024 * 1024),
        cost_estimate=pl.CostEstimate(
            flops=2 * samples * feats * columns, bytes_accessed=2 * feats * (samples + 2 * columns), transcendentals=0
        ),
    )(own, weights, parts, design)


def per_device(design, weights, probes, barrier):
    own, weights, barrier = lax.axis_index("samp").reshape(1), weights[None, :], barrier[None, :]
    own, weights, barrier = lax.optimization_barrier((own, weights, barrier))

    parts, diagonal = project(own, barrier, design, probes.T)
    parts = lax.all_to_all(parts, "feat", 0, 0, axis_index_groups=YC_GROUPS)
    parts = lax.all_to_all(resum(parts), "feat", 0, 0, axis_index_groups=ZLO_GROUPS)

    sent, up = sketch_parts(own, weights, parts, design)
    got = lax.all_to_all(sent.astype(jnp.float16), "samp", 0, 0, axis_index_groups=X_GROUPS)
    sent = got.astype(jnp.float32).sum(0).astype(jnp.float16)
    total = sent[0].astype(jnp.float32)
    for far in FAR_FIRST:
        step = [(z * X + x, (z + far) % Z * X + x) for z in range(Z) for x in range(X)]
        total += lax.ppermute(sent[far], "samp", step).astype(jnp.float32)
    return (total * up + diagonal).T


def solution(mesh):
    placed = (P("samp", "feat"), P("samp"), P("feat", None), P(("feat", "samp")))
    return jax.shard_map(
        per_device, mesh=mesh, in_specs=placed, out_specs=P(("feat", "samp"), None), check_vma=False
    )
```

```python
import jax
import jax.numpy as jnp
from jax import lax
from jax.experimental import pallas as pl
from jax.experimental.pallas import tpu as pltpu
from jax.sharding import PartitionSpec as P

X = 4
Y = 4
Z = 4
CORES = 2
CHUNKS = 2
DESIGN_MAX = 6.0
WEIGHT_MAX = 0.25
F16_TOP = 32768.0

X_GROUPS = [[z * X + x for x in range(X)] for z in range(Z)]
FAR_FIRST = (2, 1, 3)
Y_GROUPS = [[(y * Z + z) * CORES + c for y in range(Y)] for z in range(Z) for c in range(CORES)]
ZLO_GROUPS = [[(y * Z + z) * CORES + c for z in range(Z)] for y in range(Y) for c in range(CORES)]

VMEM = pl.BlockSpec(memory_space=pltpu.VMEM)


def row_of(column):
    n = column.shape[0]
    same = lax.broadcasted_iota(jnp.int32, (n, n), 0) == lax.broadcasted_iota(jnp.int32, (n, n), 1)
    return jnp.sum(jnp.where(same, jnp.broadcast_to(column, (n, n)), 0.0), axis=0, keepdims=True)


def column_of(row):
    n = row.shape[1]
    same = lax.broadcasted_iota(jnp.int32, (n, n), 0) == lax.broadcasted_iota(jnp.int32, (n, n), 1)
    return jnp.sum(jnp.where(same, jnp.broadcast_to(row, (n, n)), 0.0), axis=1, keepdims=True)


def project_kernel(own, barrier_ref, design_ref, probes_ref, out_ref, diagonal_ref, total, mass):
    step = pl.program_id(0)
    width = probes_ref.shape[1]
    half, owned = total.shape[0] // 2, diagonal_ref.shape[1]

    @pl.when(step == 0)
    def _():
        total[...] = jnp.zeros_like(total)
        mass[...] = jnp.zeros_like(mass)

    total[...] += lax.dot_general(
        design_ref[...], probes_ref[...], (((1,), (1,)), ((), ())), preferred_element_type=jnp.float32
    )
    size = jnp.abs(probes_ref[...]).astype(jnp.float32)
    for j in range(width // 128):
        mass[...] += size[:, j * 128 : (j + 1) * 128]

    blocks = width // owned

    @pl.when(step == lax.div(own[0], blocks))
    def _():
        at = pl.multiple_of(lax.rem(own[0], blocks) * owned, owned)
        diagonal_ref[...] = barrier_ref[...] * probes_ref[:, pl.ds(at, owned)].astype(jnp.float32)

    @pl.when(step == pl.num_programs(0) - 1)
    def _():
        packed = jnp.concatenate([total[:half], total[half:]], axis=1)
        row = row_of(jnp.sum(mass[...], axis=1, keepdims=True))
        row = jnp.broadcast_to(jnp.concatenate([row, row], axis=1), (8, packed.shape[1]))
        out_ref[:half] = packed
        out_ref[half:] = row


def project(own, barrier, design, probes_t):
    samples, feats = design.shape
    columns, owned = probes_t.shape[0], barrier.shape[1]
    half, width = samples // 2, feats // CHUNKS
    return pl.pallas_call(
        project_kernel,
        grid=(CHUNKS,),
        in_specs=[
            pl.BlockSpec(memory_space=pltpu.SMEM),
            pl.BlockSpec((1, owned), lambda i: (0, 0)),
            pl.BlockSpec((samples, width), lambda i: (0, i)),
            pl.BlockSpec((columns, width), lambda i: (0, i)),
        ],
        out_specs=[
            pl.BlockSpec((half + 8, 2 * columns), lambda i: (0, 0)),
            pl.BlockSpec((columns, owned), lambda i: (0, 0)),
        ],
        out_shape=[
            jax.ShapeDtypeStruct((half + 8, 2 * columns), jnp.float32),
            jax.ShapeDtypeStruct((columns, owned), jnp.float32),
        ],
        scratch_shapes=[pltpu.VMEM((samples, columns), jnp.float32), pltpu.VMEM((columns, 128), jnp.float32)],
        compiler_params=pltpu.CompilerParams(vmem_limit_bytes=60 * 1024 * 1024),
        cost_estimate=pl.CostEstimate(
            flops=2 * samples * feats * columns, bytes_accessed=2 * feats * (samples + columns), transcendentals=0
        ),
    )(own, barrier, design, probes_t)


def resum_kernel(*refs):
    out_ref = refs[-1]
    terms = [ref[i] for ref in refs[:-1] for i in range(ref.shape[0])]
    total = terms[0]
    for term in terms[1:]:
        total += term
    for i in range(out_ref.shape[0]):
        out_ref[i] = total


def resum(copies, *parts):
    size = sum(part.size for part in parts)
    return pl.pallas_call(
        resum_kernel,
        in_specs=[VMEM] * len(parts),
        out_specs=VMEM,
        out_shape=jax.ShapeDtypeStruct((copies,) + parts[0].shape[1:], jnp.float32),
        compiler_params=pltpu.CompilerParams(vmem_limit_bytes=8 * 1024 * 1024),
        cost_estimate=pl.CostEstimate(flops=size, bytes_accessed=6 * size, transcendentals=0),
    )(*parts)


def sketch_kernel(own, weights_ref, parts_ref, design_ref, out_ref, up_ref):
    columns, owned = out_ref.shape[2:]
    half = design_ref.shape[0] // 2
    own_z = lax.div(own[0], X)
    total = parts_ref[0]
    for i in range(1, parts_ref.shape[0]):
        total += parts_ref[i]
    projected = jnp.concatenate([total[:half, :columns], total[:half, columns:]], axis=0)
    scaled = (column_of(weights_ref[...]) * projected).astype(jnp.bfloat16)
    mass = column_of(total[half : half + 1, :columns])
    bound = (X * 2 * half * DESIGN_MAX * WEIGHT_MAX * DESIGN_MAX) * jnp.maximum(mass, 1e-30)
    down = F16_TOP / bound
    up_ref[...] = jnp.broadcast_to(bound / F16_TOP, up_ref.shape)
    for z in range(Z):
        for x in range(X):
            at = (z * X + x) * owned
            part = lax.dot_general(
                scaled, design_ref[:, at : at + owned], (((0,), (0,)), ((), ())), preferred_element_type=jnp.float32
            )
            out_ref[x, lax.rem(z + Z - own_z, Z)] = part * down


def sketch_parts(own, weights, parts, design):
    samples, feats = design.shape
    columns = parts.shape[2] // 2
    owned = feats // (X * Z)
    return pl.pallas_call(
        sketch_kernel,
        in_specs=[pl.BlockSpec(memory_space=pltpu.SMEM)] + [VMEM] * 3,
        out_specs=[VMEM] * 2,
        out_shape=[
            jax.ShapeDtypeStruct((X, Z, columns, owned), jnp.float32),
            jax.ShapeDtypeStruct((columns, owned), jnp.float32),
        ],
        compiler_params=pltpu.CompilerParams(vmem_limit_bytes=16 * 1024 * 1024),
        cost_estimate=pl.CostEstimate(
            flops=2 * samples * feats * columns, bytes_accessed=2 * feats * (samples + 2 * columns), transcendentals=0
        ),
    )(own, weights, parts, design)


def per_device(design, weights, probes, barrier):
    own, weights, barrier = lax.axis_index("samp").reshape(1), weights[None, :], barrier[None, :]
    own, weights, barrier = lax.optimization_barrier((own, weights, barrier))

    parts, diagonal = project(own, barrier, design, probes.T)
    parts = parts[None]
    other = lax.ppermute(parts, "feat", [(i, i ^ 1) for i in range(Y * Z * CORES)])
    parts = lax.all_to_all(jnp.broadcast_to(parts + other, (Y, *parts.shape[1:])), "feat", 0, 0, axis_index_groups=Y_GROUPS)
    parts = lax.all_to_all(resum(Z, parts), "feat", 0, 0, axis_index_groups=ZLO_GROUPS)

    sent, up = sketch_parts(own, weights, parts, design)
    got = lax.all_to_all(sent.astype(jnp.float16), "samp", 0, 0, axis_index_groups=X_GROUPS)
    sent = got.astype(jnp.float32).sum(0).astype(jnp.float16)
    total = sent[0].astype(jnp.float32)
    for far in FAR_FIRST:
        step = [(z * X + x, (z + far) % Z * X + x) for z in range(Z) for x in range(X)]
        total += lax.ppermute(sent[far], "samp", step).astype(jnp.float32)
    return (total * up + diagonal).T


def solution(mesh):
    placed = (P("samp", "feat"), P("samp"), P("feat", None), P(("feat", "samp")))
    return jax.shard_map(
        per_device, mesh=mesh, in_specs=placed, out_specs=P(("feat", "samp"), None), check_vma=False
    )
```

```python
import jax
import jax.numpy as jnp
from jax import lax
from jax.experimental import pallas as pl
from jax.experimental.pallas import tpu as pltpu
from jax.sharding import PartitionSpec as P

X = 4
Y = 4
Z = 4
CORES = 2
CHUNKS = 2
DESIGN_MAX = 6.0
WEIGHT_MAX = 0.25
F16_TOP = 32768.0

X_ORDER = (0, 2, 1, 3)
X_GROUPS = [[z * X + x for x in X_ORDER] for z in range(Z)]
FAR_FIRST = (2, 1, 3)
Y_GROUPS = [[(y * Z + z) * CORES + c for y in range(Y)] for z in range(Z) for c in range(CORES)]
ZLO_GROUPS = [[(y * Z + z) * CORES + c for z in range(Z)] for y in range(Y) for c in range(CORES)]

VMEM = pl.BlockSpec(memory_space=pltpu.VMEM)


def row_of(column):
    n = column.shape[0]
    same = lax.broadcasted_iota(jnp.int32, (n, n), 0) == lax.broadcasted_iota(jnp.int32, (n, n), 1)
    return jnp.sum(jnp.where(same, jnp.broadcast_to(column, (n, n)), 0.0), axis=0, keepdims=True)


def column_of(row):
    n = row.shape[1]
    same = lax.broadcasted_iota(jnp.int32, (n, n), 0) == lax.broadcasted_iota(jnp.int32, (n, n), 1)
    return jnp.sum(jnp.where(same, jnp.broadcast_to(row, (n, n)), 0.0), axis=1, keepdims=True)


def project_kernel(own, barrier_ref, design_ref, probes_ref, out_ref, diagonal_ref, total, mass):
    step = pl.program_id(0)
    width = probes_ref.shape[1]
    half, owned = total.shape[0] // 2, diagonal_ref.shape[1]

    @pl.when(step == 0)
    def _():
        total[...] = jnp.zeros_like(total)
        mass[...] = jnp.zeros_like(mass)

    total[...] += lax.dot_general(
        design_ref[...], probes_ref[...], (((1,), (1,)), ((), ())), preferred_element_type=jnp.float32
    )
    size = jnp.abs(probes_ref[...]).astype(jnp.float32)
    for j in range(width // 128):
        mass[...] += size[:, j * 128 : (j + 1) * 128]

    blocks = width // owned

    @pl.when(step == lax.div(own[0], blocks))
    def _():
        at = pl.multiple_of(lax.rem(own[0], blocks) * owned, owned)
        diagonal_ref[...] = barrier_ref[...] * probes_ref[:, pl.ds(at, owned)].astype(jnp.float32)

    @pl.when(step == pl.num_programs(0) - 1)
    def _():
        packed = jnp.concatenate([total[:half], total[half:]], axis=1)
        row = row_of(jnp.sum(mass[...], axis=1, keepdims=True))
        row = jnp.broadcast_to(jnp.concatenate([row, row], axis=1), (8, packed.shape[1]))
        out_ref[:half] = packed
        out_ref[half:] = row


def project(own, barrier, design, probes_t):
    samples, feats = design.shape
    columns, owned = probes_t.shape[0], barrier.shape[1]
    half, width = samples // 2, feats // CHUNKS
    return pl.pallas_call(
        project_kernel,
        grid=(CHUNKS,),
        in_specs=[
            pl.BlockSpec(memory_space=pltpu.SMEM),
            pl.BlockSpec((1, owned), lambda i: (0, 0)),
            pl.BlockSpec((samples, width), lambda i: (0, i)),
            pl.BlockSpec((columns, width), lambda i: (0, i)),
        ],
        out_specs=[
            pl.BlockSpec((half + 8, 2 * columns), lambda i: (0, 0)),
            pl.BlockSpec((columns, owned), lambda i: (0, 0)),
        ],
        out_shape=[
            jax.ShapeDtypeStruct((half + 8, 2 * columns), jnp.float32),
            jax.ShapeDtypeStruct((columns, owned), jnp.float32),
        ],
        scratch_shapes=[pltpu.VMEM((samples, columns), jnp.float32), pltpu.VMEM((columns, 128), jnp.float32)],
        compiler_params=pltpu.CompilerParams(vmem_limit_bytes=60 * 1024 * 1024),
        cost_estimate=pl.CostEstimate(
            flops=2 * samples * feats * columns, bytes_accessed=2 * feats * (samples + columns), transcendentals=0
        ),
    )(own, barrier, design, probes_t)


def resum_kernel(*refs):
    out_ref = refs[-1]
    terms = [ref[i] for ref in refs[:-1] for i in range(ref.shape[0])]
    total = terms[0]
    for term in terms[1:]:
        total += term
    for i in range(out_ref.shape[0]):
        out_ref[i] = total


def resum(copies, *parts):
    size = sum(part.size for part in parts)
    return pl.pallas_call(
        resum_kernel,
        in_specs=[VMEM] * len(parts),
        out_specs=VMEM,
        out_shape=jax.ShapeDtypeStruct((copies,) + parts[0].shape[1:], jnp.float32),
        compiler_params=pltpu.CompilerParams(vmem_limit_bytes=8 * 1024 * 1024),
        cost_estimate=pl.CostEstimate(flops=size, bytes_accessed=6 * size, transcendentals=0),
    )(*parts)


def sketch_kernel(own, weights_ref, parts_ref, design_ref, out_ref, up_ref):
    columns, owned = out_ref.shape[2:]
    half = design_ref.shape[0] // 2
    own_z = lax.div(own[0], X)
    total = parts_ref[0]
    for i in range(1, parts_ref.shape[0]):
        total += parts_ref[i]
    projected = jnp.concatenate([total[:half, :columns], total[:half, columns:]], axis=0)
    scaled = (column_of(weights_ref[...]) * projected).astype(jnp.bfloat16)
    mass = column_of(total[half : half + 1, :columns])
    bound = (X * 2 * half * DESIGN_MAX * WEIGHT_MAX * DESIGN_MAX) * jnp.maximum(mass, 1e-30)
    down = F16_TOP / bound
    up_ref[...] = jnp.broadcast_to(bound / F16_TOP, up_ref.shape)
    for z in range(Z):
        for x in range(X):
            at = (z * X + x) * owned
            part = lax.dot_general(
                scaled, design_ref[:, at : at + owned], (((0,), (0,)), ((), ())), preferred_element_type=jnp.float32
            )
            out_ref[X_ORDER.index(x), lax.rem(z + Z - own_z, Z)] = part * down


def sketch_parts(own, weights, parts, design):
    samples, feats = design.shape
    columns = parts.shape[2] // 2
    owned = feats // (X * Z)
    return pl.pallas_call(
        sketch_kernel,
        in_specs=[pl.BlockSpec(memory_space=pltpu.SMEM)] + [VMEM] * 3,
        out_specs=[VMEM] * 2,
        out_shape=[
            jax.ShapeDtypeStruct((X, Z, columns, owned), jnp.float32),
            jax.ShapeDtypeStruct((columns, owned), jnp.float32),
        ],
        compiler_params=pltpu.CompilerParams(vmem_limit_bytes=16 * 1024 * 1024),
        cost_estimate=pl.CostEstimate(
            flops=2 * samples * feats * columns, bytes_accessed=2 * feats * (samples + 2 * columns), transcendentals=0
        ),
    )(own, weights, parts, design)


def per_device(design, weights, probes, barrier):
    own, weights, barrier = lax.axis_index("samp").reshape(1), weights[None, :], barrier[None, :]
    own, weights, barrier = lax.optimization_barrier((own, weights, barrier))

    parts, diagonal = project(own, barrier, design, probes.T)
    parts = parts[None]
    other = lax.ppermute(parts, "feat", [(i, i ^ 1) for i in range(Y * Z * CORES)])
    parts = lax.all_to_all(jnp.broadcast_to(parts + other, (Y, *parts.shape[1:])), "feat", 0, 0, axis_index_groups=Y_GROUPS)
    parts = lax.all_to_all(resum(Z, parts), "feat", 0, 0, axis_index_groups=ZLO_GROUPS)

    sent, up = sketch_parts(own, weights, parts, design)
    got = lax.all_to_all(sent.astype(jnp.float16), "samp", 0, 0, axis_index_groups=X_GROUPS)
    sent = got.astype(jnp.float32).sum(0).astype(jnp.float16)
    total = sent[0].astype(jnp.float32)
    for far in FAR_FIRST:
        step = [(z * X + x, (z + far) % Z * X + x) for z in range(Z) for x in range(X)]
        total += lax.ppermute(sent[far], "samp", step).astype(jnp.float32)
    return (total * up + diagonal).T


def solution(mesh):
    placed = (P("samp", "feat"), P("samp"), P("feat", None), P(("feat", "samp")))
    return jax.shard_map(
        per_device, mesh=mesh, in_specs=placed, out_specs=P(("feat", "samp"), None), check_vma=False
    )
```

```python
import jax
import jax.numpy as jnp
from jax import lax
from jax.experimental import pallas as pl
from jax.experimental.pallas import tpu as pltpu
from jax.sharding import PartitionSpec as P

X = 4
Y = 4
Z = 4
CORES = 2
CHUNKS = 2
DESIGN_MAX = 6.0
WEIGHT_MAX = 0.25
F16_TOP = 32768.0

RING_ORDER = (0, 2, 1, 3)
X_GROUPS = [[z * X + x for x in RING_ORDER] for z in range(Z)]
FAR_FIRST = (2, 1, 3)
Y_GROUPS = [[(y * Z + z) * CORES + c for y in RING_ORDER] for z in range(Z) for c in range(CORES)]
ZLO_GROUPS = [[(y * Z + z) * CORES + c for z in range(Z)] for y in range(Y) for c in range(CORES)]

VMEM = pl.BlockSpec(memory_space=pltpu.VMEM)


def row_of(column):
    n = column.shape[0]
    same = lax.broadcasted_iota(jnp.int32, (n, n), 0) == lax.broadcasted_iota(jnp.int32, (n, n), 1)
    return jnp.sum(jnp.where(same, jnp.broadcast_to(column, (n, n)), 0.0), axis=0, keepdims=True)


def column_of(row):
    n = row.shape[1]
    same = lax.broadcasted_iota(jnp.int32, (n, n), 0) == lax.broadcasted_iota(jnp.int32, (n, n), 1)
    return jnp.sum(jnp.where(same, jnp.broadcast_to(row, (n, n)), 0.0), axis=1, keepdims=True)


def project_kernel(own, barrier_ref, design_ref, probes_ref, out_ref, diagonal_ref, total, mass):
    step = pl.program_id(0)
    width = probes_ref.shape[1]
    half, owned = total.shape[0] // 2, diagonal_ref.shape[1]

    @pl.when(step == 0)
    def _():
        total[...] = jnp.zeros_like(total)
        mass[...] = jnp.zeros_like(mass)

    total[...] += lax.dot_general(
        design_ref[...], probes_ref[...], (((1,), (1,)), ((), ())), preferred_element_type=jnp.float32
    )
    size = jnp.abs(probes_ref[...]).astype(jnp.float32)
    for j in range(width // 128):
        mass[...] += size[:, j * 128 : (j + 1) * 128]

    blocks = width // owned

    @pl.when(step == lax.div(own[0], blocks))
    def _():
        at = pl.multiple_of(lax.rem(own[0], blocks) * owned, owned)
        diagonal_ref[...] = barrier_ref[...] * probes_ref[:, pl.ds(at, owned)].astype(jnp.float32)

    @pl.when(step == pl.num_programs(0) - 1)
    def _():
        packed = jnp.concatenate([total[:half], total[half:]], axis=1)
        row = row_of(jnp.sum(mass[...], axis=1, keepdims=True))
        row = jnp.broadcast_to(jnp.concatenate([row, row], axis=1), (8, packed.shape[1]))
        out_ref[:half] = packed
        out_ref[half:] = row


def project(own, barrier, design, probes_t):
    samples, feats = design.shape
    columns, owned = probes_t.shape[0], barrier.shape[1]
    half, width = samples // 2, feats // CHUNKS
    return pl.pallas_call(
        project_kernel,
        grid=(CHUNKS,),
        in_specs=[
            pl.BlockSpec(memory_space=pltpu.SMEM),
            pl.BlockSpec((1, owned), lambda i: (0, 0)),
            pl.BlockSpec((samples, width), lambda i: (0, i)),
            pl.BlockSpec((columns, width), lambda i: (0, i)),
        ],
        out_specs=[
            pl.BlockSpec((half + 8, 2 * columns), lambda i: (0, 0)),
            pl.BlockSpec((columns, owned), lambda i: (0, 0)),
        ],
        out_shape=[
            jax.ShapeDtypeStruct((half + 8, 2 * columns), jnp.float32),
            jax.ShapeDtypeStruct((columns, owned), jnp.float32),
        ],
        scratch_shapes=[pltpu.VMEM((samples, columns), jnp.float32), pltpu.VMEM((columns, 128), jnp.float32)],
        compiler_params=pltpu.CompilerParams(vmem_limit_bytes=60 * 1024 * 1024),
        cost_estimate=pl.CostEstimate(
            flops=2 * samples * feats * columns, bytes_accessed=2 * feats * (samples + columns), transcendentals=0
        ),
    )(own, barrier, design, probes_t)


def resum_kernel(*refs):
    out_ref = refs[-1]
    terms = [ref[i] for ref in refs[:-1] for i in range(ref.shape[0])]
    total = terms[0]
    for term in terms[1:]:
        total += term
    for i in range(out_ref.shape[0]):
        out_ref[i] = total


def resum(copies, *parts):
    size = sum(part.size for part in parts)
    return pl.pallas_call(
        resum_kernel,
        in_specs=[VMEM] * len(parts),
        out_specs=VMEM,
        out_shape=jax.ShapeDtypeStruct((copies,) + parts[0].shape[1:], jnp.float32),
        compiler_params=pltpu.CompilerParams(vmem_limit_bytes=8 * 1024 * 1024),
        cost_estimate=pl.CostEstimate(flops=size, bytes_accessed=6 * size, transcendentals=0),
    )(*parts)


def sketch_kernel(own, weights_ref, parts_ref, design_ref, out_ref, up_ref):
    columns, owned = out_ref.shape[2:]
    half = design_ref.shape[0] // 2
    own_z = lax.div(own[0], X)
    total = parts_ref[0]
    for i in range(1, parts_ref.shape[0]):
        total += parts_ref[i]
    projected = jnp.concatenate([total[:half, :columns], total[:half, columns:]], axis=0)
    scaled = (column_of(weights_ref[...]) * projected).astype(jnp.bfloat16)
    mass = column_of(total[half : half + 1, :columns])
    bound = (X * 2 * half * DESIGN_MAX * WEIGHT_MAX * DESIGN_MAX) * jnp.maximum(mass, 1e-30)
    down = F16_TOP / bound
    up_ref[...] = jnp.broadcast_to(bound / F16_TOP, up_ref.shape)
    for z in range(Z):
        for x in range(X):
            at = (z * X + x) * owned
            part = lax.dot_general(
                scaled, design_ref[:, at : at + owned], (((0,), (0,)), ((), ())), preferred_element_type=jnp.float32
            )
            out_ref[RING_ORDER.index(x), lax.rem(z + Z - own_z, Z)] = part * down


def sketch_parts(own, weights, parts, design):
    samples, feats = design.shape
    columns = parts.shape[2] // 2
    owned = feats // (X * Z)
    return pl.pallas_call(
        sketch_kernel,
        in_specs=[pl.BlockSpec(memory_space=pltpu.SMEM)] + [VMEM] * 3,
        out_specs=[VMEM] * 2,
        out_shape=[
            jax.ShapeDtypeStruct((X, Z, columns, owned), jnp.float32),
            jax.ShapeDtypeStruct((columns, owned), jnp.float32),
        ],
        compiler_params=pltpu.CompilerParams(vmem_limit_bytes=16 * 1024 * 1024),
        cost_estimate=pl.CostEstimate(
            flops=2 * samples * feats * columns, bytes_accessed=2 * feats * (samples + 2 * columns), transcendentals=0
        ),
    )(own, weights, parts, design)


def per_device(design, weights, probes, barrier):
    own, weights, barrier = lax.axis_index("samp").reshape(1), weights[None, :], barrier[None, :]
    own, weights, barrier = lax.optimization_barrier((own, weights, barrier))

    parts, diagonal = project(own, barrier, design, probes.T)
    parts = parts[None]
    other = lax.ppermute(parts, "feat", [(i, i ^ 1) for i in range(Y * Z * CORES)])
    parts = lax.all_to_all(jnp.broadcast_to(parts + other, (Y, *parts.shape[1:])), "feat", 0, 0, axis_index_groups=Y_GROUPS)
    parts = lax.all_to_all(resum(Z, parts), "feat", 0, 0, axis_index_groups=ZLO_GROUPS)

    sent, up = sketch_parts(own, weights, parts, design)
    got = lax.all_to_all(sent.astype(jnp.float16), "samp", 0, 0, axis_index_groups=X_GROUPS)
    sent = got.astype(jnp.float32).sum(0).astype(jnp.float16)
    total = sent[0].astype(jnp.float32)
    for far in FAR_FIRST:
        step = [(z * X + x, (z + far) % Z * X + x) for z in range(Z) for x in range(X)]
        total += lax.ppermute(sent[far], "samp", step).astype(jnp.float32)
    return (total * up + diagonal).T


def solution(mesh):
    placed = (P("samp", "feat"), P("samp"), P("feat", None), P(("feat", "samp")))
    return jax.shard_map(
        per_device, mesh=mesh, in_specs=placed, out_specs=P(("feat", "samp"), None), check_vma=False
    )
```
